256 devices in a mesh: dp: 16 (over z, core), tp: 16 (over y, x).
Axes of the slice: x: 4, y: 4, z: 8, core: 2. Of those that a mesh axis runs over, the one named last changes fastest.
Arguments:
- queries: bfloat16 [256, 128, 576], P(('dp', 'tp')), may hold values from -14 to 14
- new_latent: bfloat16 [256, 576], P(('dp', 'tp')), may hold values from -6 to 6
- latent_cache: bfloat16 [256, 1024, 576], P(('dp', 'tp')), may hold values from -6 to 6
- cached_lengths: int32 [256], P(('dp', 'tp')), may hold values from 1 to 1024, as said below
- value_up: bfloat16 [128, 512, 128], P('tp'), may hold values from -0.25 to 0.25
- out_weight: bfloat16 [16384, 7168], P('tp', 'dp'), may hold values from -0.046875 to 0.046875
- residual_in: bfloat16 [256, 7168], P('tp', 'dp'), may hold values from -0.3125 to 0.3125
- norm_gain: float32 [7168], P('dp'), may hold values from 0.5 to 1.5
- gate_weight: bfloat16 [7168, 18432], P('dp', 'tp'), may hold values from -0.0625 to 0.0625
- up_weight: bfloat16 [7168, 18432], P('dp', 'tp'), may hold values from -0.0625 to 0.0625
- down_weight: bfloat16 [18432, 7168], P('tp', 'dp'), may hold values from -0.046875 to 0.046875
Outputs:
- layer_out: bfloat16 [256, 7168], P('tp', 'dp')
The draws below stay inside these ranges and needn't reach their ends.
Inputs may be any that keep to these rules, and one draw needn't show every extreme that they name: `cached_lengths`: cached positions of each request; some request has all 1024.
All inputs are finite; a program needn't handle non-finite values.
Results may differ from the reference program's by a relative error of at most 0.02.
Values may be sent and summed in bfloat16 or wider, within the bound.
A program may use at most 64 MiB of HBM per device.

```python
import jax
import jax.numpy as jnp
from jax import lax

D = 7168
FF = 18432
HEADS = 128
LATENT = 512
ROPE = 64
NOPE = 128
HEAD_V = 128
R_SLOTS = 1
CACHE = 1024
ROWS = 256


def first_pair(key):
    key_normal = jax.random.fold_in(jax.random.fold_in(key, 7), 0)
    shape = (ROWS, 2, LATENT + ROPE)
    normal_part = jax.random.truncated_normal(key_normal, -6.0, 6.0, shape, jnp.float32)
    return normal_part


def draw_latent_cache(key, part):
    leading = first_pair(key)
    key = jax.random.fold_in(key, 11)
    key_normal = jax.random.fold_in(key, 0)
    shape = (ROWS, CACHE - 2, LATENT + ROPE)
    normal_part = jax.random.truncated_normal(key_normal, -6.0, 6.0, shape, jnp.float32)
    rest = normal_part
    return jnp.concatenate([leading, rest], axis=1).astype(jnp.bfloat16)


def draw_queries(key, part):
    key = jax.random.fold_in(key, 13)
    base_draw = jax.random.truncated_normal(key, -6.0, 6.0, (ROWS, HEADS, LATENT + ROPE), jnp.float32)
    return base_draw.astype(jnp.bfloat16)


def draw_cached_lengths(key, part):
    key = jax.random.fold_in(key, 17)
    key_each, key_device, key_high, key_low = jax.random.split(key, 4)
    uniform_len = jax.random.randint(key_each, (ROWS,), 1, CACHE + 1)
    factor = jax.random.randint(key_device, (ROWS // R_SLOTS,), 1, 9)
    factor = jnp.repeat(factor, R_SLOTS)
    lengths = jnp.maximum(1, uniform_len * factor // 8)
    high_row = jax.random.randint(key_high, (), 0, ROWS)
    low_row = (high_row + 1 + jax.random.randint(key_low, (), 0, ROWS - 1)) % ROWS
    row_index = jnp.arange(ROWS)
    lengths = jnp.where(row_index == high_row, CACHE, jnp.where(row_index == low_row, 1, lengths))
    return lengths.astype(jnp.int32)


def level_of(rng, shape, cuts, smallest, largest):
    gain = 1.0
    for axis_at, parts in cuts:
        heights = jax.random.uniform(jax.random.fold_in(jax.random.fold_in(rng, 6), axis_at), (parts,), jnp.float32, smallest / len(cuts), largest / len(cuts))
        gain = gain * jnp.repeat(jnp.exp(heights), shape[axis_at] // parts).reshape((-1,) + (1,) * (len(shape) - 1 - axis_at))
    return gain


def centred(own_key, shape, spread, limit, cuts=(), held_as=jnp.bfloat16):
    loudness = level_of(own_key, shape, cuts, -0.22, 0.18) if cuts else 1.0
    entries = jax.random.normal(own_key, shape, jnp.float32) * spread * loudness
    return jnp.minimum(jnp.maximum(entries, -limit), limit).astype(held_as)


def setup_inputs(seed: int = 0) -> dict:
    streams_of = jax.random.split(jax.random.key(seed), 12)
    return {
        "queries": draw_queries(jax.random.fold_in(streams_of[11], 71), 0),
        "new_latent": centred(streams_of[1], (ROWS, LATENT + ROPE), 1.0, 6.0, ((0, 256),)),
        "latent_cache": draw_latent_cache(jax.random.fold_in(streams_of[11], 71), 0),
        "cached_lengths": draw_cached_lengths(jax.random.fold_in(streams_of[11], 71), 0),
        "value_up": centred(streams_of[4], (HEADS, LATENT, HEAD_V), LATENT ** -0.5, 0.25, ((0, 16),)),
        "out_weight": centred(streams_of[5], (HEADS * HEAD_V, D), (HEADS * HEAD_V) ** -0.5, 0.046875, ((0, 16), (1, 16))),
        "residual_in": centred(streams_of[6], (ROWS, D), 0.05, 0.3125, ((0, 16), (1, 16))),
        "norm_gain": jnp.clip(1.0 + 0.1 * jax.random.normal(streams_of[7], (D,), jnp.float32), 0.5, 1.5),
        "gate_weight": centred(streams_of[8], (D, FF), D ** -0.5, 0.0625, ((0, 16), (1, 16))),
        "up_weight": centred(streams_of[9], (D, FF), D ** -0.5, 0.0625, ((0, 16), (1, 16))),
        "down_weight": centred(streams_of[10], (FF, D), FF ** -0.5, 0.046875, ((0, 16), (1, 16))),
    }


def attend_one(packed):
    query, fresh, cache_rows, length = packed
    score_scale = (NOPE + ROPE) ** (-0.5)
    scores = jnp.dot(query, cache_rows.T, preferred_element_type=jnp.float32) * score_scale
    position = jnp.arange(CACHE)
    scores = jnp.where(position[None, :] < length, scores, -1e+30)
    own_score = jnp.dot(query, fresh, preferred_element_type=jnp.float32) * score_scale
    top_score = jnp.maximum(lax.optimization_barrier(jnp.max(scores, axis=1)), own_score)
    weights = jnp.exp(scores - top_score[:, None])
    own_weight = jnp.exp(own_score - top_score)
    total_weight = lax.optimization_barrier(jnp.sum(weights, axis=1)) + own_weight
    rounded = weights.astype(jnp.bfloat16)
    summed = jnp.dot(rounded, cache_rows[:, :LATENT], preferred_element_type=jnp.float32)
    summed = summed + own_weight[:, None] * fresh[:LATENT].astype(jnp.float32)[None, :]
    return (summed / total_weight[:, None]).astype(jnp.bfloat16)

def reference(queries, new_latent, latent_cache, cached_lengths, value_up, out_weight, residual_in, norm_gain, gate_weight, up_weight, down_weight):
    head_latent = lax.map(attend_one, (queries, new_latent, latent_cache, cached_lengths))
    values = jnp.einsum('rhc,hcv->rhv', head_latent.astype(jnp.float32), value_up.astype(jnp.float32))
    values = values.astype(jnp.bfloat16).reshape(ROWS, HEADS * HEAD_V)
    stream = residual_in.astype(jnp.float32) + jnp.dot(values, out_weight, preferred_element_type=jnp.float32)
    mean_square = lax.optimization_barrier(jnp.mean(stream * stream, axis=1))
    normed = (stream * lax.rsqrt(mean_square + 1e-06)[:, None] * norm_gain[None, :]).astype(jnp.bfloat16)
    gate_sum = jnp.dot(normed, gate_weight, preferred_element_type=jnp.float32)
    up_sum = jnp.dot(normed, up_weight, preferred_element_type=jnp.float32)
    hidden = (jax.nn.silu(gate_sum) * up_sum).astype(jnp.bfloat16)
    lowered = jnp.dot(hidden, down_weight, preferred_element_type=jnp.float32)
    return (stream + lowered).astype(jnp.bfloat16)
```

```python
import jax
import jax.numpy as jnp
from jax import lax
from jax.experimental import pallas as pl
from jax.experimental.pallas import tpu as pltpu
from jax.sharding import PartitionSpec as P

D = 7168
HEADS = 128
LATENT = 512
KEY = 576
CACHE = 1024
SCALE = (128 + 64) ** (-0.5)
PLANE = 16
CHIPS = 8
ROWS = 16
OWN_HEADS = 8
VALUES = 1024
FEAT = 448
PAD = 512
UNITS = 1152
WIDE = 2 * UNITS + 128
F32 = jnp.float32
BF16 = jnp.bfloat16
MESH = pl.DeviceIdType.MESH


def kernel(
    queries,
    fresh,
    cache,
    length,
    value_up,
    out_weight,
    residual,
    gain,
    gate_weight,
    up_weight,
    down_weight,
    out,
    q_v,
    k_v,
    vu_v,
    ow_v,
    gu_v,
    dw_v,
    head_out,
    head_in,
    val,
    o_out,
    o_in,
    x_out,
    x_in,
    part,
    ring_l,
    ring_s,
    got_l,
    got_s,
    hid,
    d_out,
    d_in,
    load_sem,
    swap_send,
    swap_recv,
    head_send,
    head_recv,
    val_send,
    val_recv,
    o_send,
    o_recv,
    x_send,
    x_recv,
    ring_send,
    ring_recv,
    hid_send,
    hid_recv,
    d_send,
    d_recv,
):
    dp, tp = lax.axis_index("dp"), lax.axis_index("tp")
    z, core = lax.div(dp, 2), lax.rem(dp, 2)
    way = 1 - 2 * core
    tp_chip, tp_core = lax.div(tp, 2), lax.rem(tp, 2)
    sibling = (dp + way, tp)

    def chip(steps):
        return lax.rem(z + way * steps + CHIPS, CHIPS)

    ahead = (2 * chip(1) + core, tp)
    behind = (2 * chip(-1) + core, tp)

    def column(steps):
        return lax.rem(tp + steps, PLANE)

    sent = []

    def push(src, dst, send_sem, recv_sem, device):
        copy = pltpu.make_async_remote_copy(src, dst, send_sem, recv_sem, device, MESH)
        copy.start()
        sent.append(copy)
        return copy

    def finish():
        for copy in sent:
            copy.wait_send()

    def load(src, dst, i):
        copy = pltpu.make_async_copy(src, dst, load_sem.at[i])
        copy.start()
        return copy

    gu_v[FEAT:PAD, :] = jnp.zeros((PAD - FEAT, WIDE), BF16)
    gu_v[PAD + FEAT :, :] = jnp.zeros((PAD - FEAT, WIDE), BF16)
    gu_v[:, 2 * UNITS :] = jnp.zeros((2 * PAD, WIDE - 2 * UNITS), BF16)
    row = lax.broadcasted_iota(jnp.int32, (16, 128), 0)
    ones = jnp.where(row < 2, 1.0, 0.0).astype(BF16)
    gu_v[FEAT : FEAT + 16, 2 * UNITS :] = ones
    gu_v[PAD + FEAT : PAD + FEAT + 16, 2 * UNITS :] = ones

    load_q = load(queries.at[0], q_v, 0)
    load_k = load(cache.at[0], k_v, 1)

    barrier = pltpu.get_barrier_semaphore()
    for i in range(1, PLANE):
        pl.semaphore_signal(barrier, inc=1, device_id=(dp, column(i)), device_id_type=MESH)
    for i in range(PLANE):
        pl.semaphore_signal(
            barrier, inc=1, device_id=(dp + way, column(i)), device_id_type=MESH
        )
    for device in (ahead, behind):
        pl.semaphore_signal(barrier, inc=1, device_id=device, device_id_type=MESH)

    load_vu = [
        load(value_up.at[h], vu_v.at[:, pl.ds(128 * h, 128)], 2 + h) for h in range(OWN_HEADS)
    ]
    mine = pl.ds(pl.multiple_of(core * PAD, PAD), FEAT)
    weights = [
        (out_weight, ow_v.at[core]),
        (gate_weight, gu_v.at[mine, pl.ds(0, UNITS)]),
        (up_weight, gu_v.at[mine, pl.ds(UNITS, UNITS)]),
        (down_weight, dw_v.at[core]),
    ]
    load_w = [load(src, dst, 10 + i) for i, (src, dst) in enumerate(weights)]

    load_q.wait()
    load_k.wait()
    q = q_v[...]
    scores = lax.dot_general(
        q, k_v[...], (((1,), (1,)), ((), ())), preferred_element_type=F32
    )
    pl.semaphore_wait(barrier, 2 * PLANE + 1)
    swaps = [
        push(src, dst, swap_send.at[i], swap_recv.at[i], sibling)
        for i, (src, dst) in enumerate(weights)
    ]
    position = lax.broadcasted_iota(jnp.int32, (HEADS, CACHE), 1)
    scores = jnp.where(position < length[0], scores * SCALE, -1e30)
    new = fresh[...].astype(F32)
    own = jnp.sum(q.astype(F32) * new, axis=1, keepdims=True) * SCALE
    top = jnp.maximum(own, jnp.max(scores, axis=1, keepdims=True))
    weight = jnp.exp(scores - top)
    own_weight = jnp.exp(own - top)
    total = jnp.sum(weight, axis=1, keepdims=True) + own_weight
    summed = jnp.dot(weight.astype(BF16), k_v[:, :LATENT], preferred_element_type=F32)
    latent = ((summed + own_weight * new[:, :LATENT]) / total).reshape(PLANE, OWN_HEADS, LATENT)
    half = LATENT // 2
    head_out[...] = jnp.concatenate([latent[:, :, :half], latent[:, :, half:]], axis=1).astype(BF16)

    for i in range(1, PLANE):
        push(
            head_out.at[column(i)],
            head_in.at[tp],
            head_send.at[i],
            head_recv.at[i],
            (dp, column(i)),
        )
    head_in[tp] = head_out[tp]
    for copy in load_vu:
        copy.wait()
    for i in range(1, PLANE):
        slot = head_in.at[column(PLANE - i)]
        pltpu.make_async_remote_copy(
            slot, slot, head_send.at[i], head_recv.at[i], (dp, tp), MESH
        ).wait_recv()


    wide = head_in[...].astype(F32)
    latents = jnp.concatenate([wide[:, :OWN_HEADS], wide[:, OWN_HEADS:]], axis=2)
    latents = latents.reshape(PLANE * OWN_HEADS, LATENT).astype(BF16)
    products = jnp.dot(latents, vu_v[...], preferred_element_type=F32)
    row_head = lax.broadcasted_iota(jnp.int32, products.shape, 0) & (OWN_HEADS - 1)
    column_head = lax.broadcasted_iota(jnp.int32, products.shape, 1) >> 7
    products = jnp.where(row_head == column_head, products, 0.0).astype(BF16)
    to_row = lax.broadcasted_iota(jnp.int32, (ROWS, PLANE * OWN_HEADS), 0)
    from_row = lax.broadcasted_iota(jnp.int32, (ROWS, PLANE * OWN_HEADS), 1) >> 3
    pick = jnp.where(to_row == from_row, 1.0, 0.0).astype(BF16)
    val[z] = jnp.dot(pick, products, preferred_element_type=F32).astype(BF16)

    def gather(buf, send_sem, recv_sem, use):
        def step(slot, i, device):
            return push(buf.at[slot], buf.at[slot], send_sem.at[i], recv_sem.at[i], device)

        def arrived(slot, i):
            ref = buf.at[slot]
            pltpu.make_async_remote_copy(
                ref, ref, send_sem.at[i], recv_sem.at[i], ahead, MESH
            ).wait_recv()

        step(z, 0, ahead)
        step(z, 4, behind)
        use([z], 0)
        for j in range(1, 5):
            arrived(chip(-j), j - 1)
            if j < 4:
                step(chip(-j), j, ahead)
                arrived(chip(j), 3 + j)
                if j < 3:
                    step(chip(j), 4 + j, behind)
            use([chip(-j), chip(j)] if j < 4 else [chip(-j)], 2 * j - 1)

    def project(buf, w, dst_out, dst_in, send_sem, recv_sem):
        def use(chips, first):
            rows = jnp.concatenate([buf[c] for c in chips], axis=0) if len(chips) > 1 else buf[chips[0]]
            for to in range(2):
                sums = jnp.dot(rows, w[to], preferred_element_type=F32).astype(BF16)
                for n, c in enumerate(chips):
                    dst_out[c, to, :, :FEAT] = sums[n * ROWS : (n + 1) * ROWS]
            for n, c in enumerate(chips):
                owner = 2 * c + core
                i = first + n
                push(
                    dst_out.at[c, 1 - core],
                    dst_in.at[tp],
                    send_sem.at[i, 0],
                    recv_sem.at[tp],
                    (dp + way, owner),
                )

                @pl.when(owner != tp)
                def _():
                    pltpu.make_async_remote_copy(
                        dst_out.at[c, core],
                        dst_in.at[tp],
                        send_sem.at[i, 1],
                        recv_sem.at[tp],
                        (dp, owner),
                        MESH,
                    ).start()

                @pl.when(owner == tp)
                def _():
                    dst_in[tp] = dst_out[c, core]

        return use

    def project_sent(dst_out, send_sem):
        for i in range(CHIPS):
            c = z if i == 0 else chip(-((i + 1) // 2)) if i % 2 else chip(i // 2)

            @pl.when(2 * c + core != tp)
            def _():
                ref = dst_out.at[c, core]
                pltpu.make_async_remote_copy(
                    ref, ref, send_sem.at[i, 1], send_sem.at[i, 1], ahead, MESH
                ).wait_send()

    def collect(dst_in, recv_sem):
        for i in range(PLANE):
            src = column(i)

            def arrived():
                ref = dst_in.at[src]
                pltpu.make_async_remote_copy(
                    ref, ref, recv_sem.at[src], recv_sem.at[src], ahead, MESH
                ).wait_recv()

            if i == 0:
                pl.when(core != tp_core)(arrived)
            else:
                arrived()
        return jnp.sum(dst_in[...].astype(F32), axis=0)

    load_w[0].wait()
    swaps[0].wait_recv()
    gather(val, val_send, val_recv, project(val, ow_v, o_out, o_in, o_send, o_recv))
    attention = collect(o_in, o_recv)
    stream = residual[...].astype(F32) + attention[:, :FEAT]

    squares = jnp.sum(stream * stream, axis=1, keepdims=True)
    high = squares.astype(BF16).astype(F32)
    lane = lax.broadcasted_iota(jnp.int32, (ROWS, PAD - FEAT), 1)
    extra = jnp.where(lane == 0, high, jnp.where(lane == 1, squares - high, 0.0))
    x_out[:, :FEAT] = (stream * gain[...]).astype(BF16)
    x_out[:, FEAT:] = extra.astype(BF16)
    x_slot = x_in.at[tp_chip, core]
    for i in range(1, PLANE):
        push(
            x_out,
            x_slot,
            x_send.at[i],
            x_recv.at[tp_chip, core],
            (2 * z + tp_core, column(i)),
        )

    def x_to_sibling():
        return pltpu.make_async_remote_copy(
            x_out, x_slot, x_send.at[0], x_recv.at[tp_chip, core], sibling, MESH
        )

    @pl.when(tp_core != core)
    def _():
        x_to_sibling().start()

    @pl.when(tp_core == core)
    def _():
        x_in[tp_chip, core] = x_out[...]

    def x_wait(c):
        for src in range(2):

            @pl.when(jnp.logical_or(2 * c + core != tp, core != src))
            def _():
                ref = x_in.at[c, src]
                pltpu.make_async_remote_copy(
                    ref, ref, x_recv.at[c, src], x_recv.at[c, src], ahead, MESH
                ).wait_recv()

    def gate_up(i):
        to_l, to_s = chip(4 - i), chip(i - 3)
        x_wait(to_l)
        x_wait(to_s)
        rows = jnp.concatenate(
            [
                jnp.concatenate([x_in[to_l, 0], x_in[to_l, 1]], axis=1),
                jnp.concatenate([x_in[to_s, 0], x_in[to_s, 1]], axis=1),
            ],
            axis=0,
        )
        part[i] = jnp.dot(rows, gu_v[...], preferred_element_type=F32)

    cuts = [(0, 1280), (1280, 1152)]

    def ring(out_buf, in_buf, i, n, side, device):
        lo, size = cuts[n]
        mine = part[i, side * ROWS : (side + 1) * ROWS, lo : lo + size]
        if i > 0:
            ref = in_buf.at[i - 1, :, pl.ds(lo, size)]
            pltpu.make_async_remote_copy(
                ref, ref, ring_send.at[side, i - 1, n], ring_recv.at[side, i - 1, n], ahead, MESH
            ).wait_recv()
            mine = mine + in_buf[i - 1, :, lo : lo + size].astype(F32)
        out_buf[i, :, lo : lo + size] = mine.astype(BF16)
        push(
            out_buf.at[i, :, pl.ds(lo, size)],
            in_buf.at[i, :, pl.ds(lo, size)],
            ring_send.at[side, i, n],
            ring_recv.at[side, i, n],
            device,
        )

    for copy in load_w[1:3]:
        copy.wait()
    for copy in swaps[1:3]:
        copy.wait_recv()
    for i in range(4):
        gate_up(i)
        for n in range(len(cuts)):
            ring(ring_l, got_l, i, n, 0, ahead)
            if i < 3:
                ring(ring_s, got_s, i, n, 1, behind)
    whole = []
    for n, (lo, size) in enumerate(cuts):
        mine = part[3, ROWS:, lo : lo + size]
        for side, i, buf in ((1, 2, got_s), (0, 3, got_l)):
            ref = buf.at[i, :, pl.ds(lo, size)]
            pltpu.make_async_remote_copy(
                ref, ref, ring_send.at[side, i, n], ring_recv.at[side, i, n], ahead, MESH
            ).wait_recv()
            mine = mine + buf[i, :, lo : lo + size].astype(F32)
        whole.append(mine)
    whole = jnp.concatenate(whole, axis=1)
    inverse = lax.rsqrt(whole[:, 2 * UNITS : 2 * UNITS + 1] * (1.0 / D) + 1e-06)
    gate = whole[:, :UNITS] * inverse
    up = whole[:, UNITS : 2 * UNITS] * inverse
    hid[z] = (gate / (1.0 + jnp.exp(-gate)) * up).astype(BF16)

    load_w[3].wait()
    swaps[3].wait_recv()
    gather(hid, hid_send, hid_recv, project(hid, dw_v, d_out, d_in, d_send, d_recv))
    lowered = collect(d_in, d_recv)
    out[...] = (stream + lowered[:, :FEAT]).astype(BF16)

    finish()
    project_sent(o_out, o_send)
    project_sent(d_out, d_send)

    @pl.when(tp_core != core)
    def _():
        x_to_sibling().wait_send()


def layer(
    queries,
    new_latent,
    latent_cache,
    cached_lengths,
    value_up,
    out_weight,
    residual_in,
    norm_gain,
    gate_weight,
    up_weight,
    down_weight,
):
    anywhere = pl.BlockSpec(memory_space=pl.ANY)
    vmem = pl.BlockSpec(memory_space=pltpu.VMEM)
    smem = pl.BlockSpec(memory_space=pltpu.SMEM)
    dma = pltpu.SemaphoreType.DMA
    return pl.pallas_call(
        kernel,
        out_shape=jax.ShapeDtypeStruct((ROWS, FEAT), BF16),
        in_specs=[
            anywhere,
            vmem,
            anywhere,
            smem,
            anywhere,
            anywhere,
            vmem,
            vmem,
            anywhere,
            anywhere,
            anywhere,
        ],
        out_specs=vmem,
        scratch_shapes=[
            pltpu.VMEM((HEADS, KEY), BF16),
            pltpu.VMEM((CACHE, KEY), BF16),
            pltpu.VMEM((LATENT, VALUES), BF16),
            pltpu.VMEM((2, VALUES, FEAT), BF16),
            pltpu.VMEM((2 * PAD, WIDE), BF16),
            pltpu.VMEM((2, UNITS, FEAT), BF16),
            pltpu.VMEM((PLANE, ROWS, LATENT // 2), BF16),
            pltpu.VMEM((PLANE, ROWS, LATENT // 2), BF16),
            pltpu.VMEM((CHIPS, ROWS, VALUES), BF16),
            pltpu.VMEM((CHIPS, 2, ROWS, PAD), BF16),
            pltpu.VMEM((PLANE, ROWS, PAD), BF16),
            pltpu.VMEM((ROWS, PAD), BF16),
            pltpu.VMEM((CHIPS, 2, ROWS, PAD), BF16),
            pltpu.VMEM((4, 2 * ROWS, WIDE), F32),
            pltpu.VMEM((4, ROWS, WIDE), BF16),
            pltpu.VMEM((3, ROWS, WIDE), BF16),
            pltpu.VMEM((4, ROWS, WIDE), BF16),
            pltpu.VMEM((3, ROWS, WIDE), BF16),
            pltpu.VMEM((CHIPS, ROWS, UNITS), BF16),
            pltpu.VMEM((CHIPS, 2, ROWS, PAD), BF16),
            pltpu.VMEM((PLANE, ROWS, PAD), BF16),
            dma((14,)),
            dma((4,)),
            dma((4,)),
            dma((PLANE,)),
            dma((PLANE,)),
            dma((7,)),
            dma((7,)),
            dma((CHIPS, 2)),
            dma((PLANE,)),
            dma((PLANE,)),
            dma((CHIPS, 2)),
            dma((2, 4, 2)),
            dma((2, 4, 2)),
            dma((7,)),
            dma((7,)),
            dma((CHIPS, 2)),
            dma((PLANE,)),
        ],
        compiler_params=pltpu.CompilerParams(
            collective_id=0, has_side_effects=True, vmem_limit_bytes=48 * 1024 * 1024
        ),
    )(
        queries,
        new_latent,
        latent_cache,
        cached_lengths,
        value_up,
        out_weight,
        residual_in,
        norm_gain.reshape(1, FEAT),
        gate_weight,
        up_weight,
        down_weight,
    )


def solution(mesh):
    in_specs = (
        P(("dp", "tp"), None, None),
        P(("dp", "tp"), None),
        P(("dp", "tp"), None, None),
        P(("dp", "tp")),
        P("tp", None, None),
        P("tp", "dp"),
        P("tp", "dp"),
        P("dp"),
        P("dp", "tp"),
        P("dp", "tp"),
        P("tp", "dp"),
    )
    return jax.shard_map(
        layer, mesh=mesh, in_specs=in_specs, out_specs=P("tp", "dp"), check_vma=False
    )
```

```python
import jax
import jax.numpy as jnp
from jax import lax
from jax.experimental import pallas as pl
from jax.experimental.pallas import tpu as pltpu
from jax.sharding import PartitionSpec as P

D = 7168
HEADS = 128
LATENT = 512
KEY = 576
CACHE = 1024
SCALE = (128 + 64) ** (-0.5)
PLANE = 16
CHIPS = 8
ROWS = 16
OWN_HEADS = 8
VALUES = 1024
FEAT = 448
PAD = 512
UNITS = 1152
WIDE = 2 * UNITS + 128
F32 = jnp.float32
BF16 = jnp.bfloat16
MESH = pl.DeviceIdType.MESH
SEND_ORDER = (4, 3, 5, 2, 6, 1, 7)
GROUPS = ((0,), (1, 7), (2, 6), (3, 5, 4))
CUTS = ((0, 1280), (1280, WIDE - 1280))


def by_columns(a, b):
    return lax.dot_general(a, b, (((1,), (1,)), ((), ())), preferred_element_type=F32)


def kernel(
    queries,
    fresh,
    cache,
    length,
    value_up,
    out_weight,
    residual,
    gain,
    gate_weight,
    up_weight,
    down_weight,
    out,
    q_v,
    k_v,
    fresh_v,
    residual_v,
    gain_v,
    vu_v,
    ow_v,
    gu_v,
    dw_v,
    head_out,
    head_in,
    val,
    o_out,
    o_in,
    x_out,
    x_in,
    part,
    sum_out,
    sum_in,
    hid,
    d_out,
    d_in,
    load_sem,
    swap_send,
    swap_recv,
    head_sem,
    val_sem,
    o_sem,
    x_sem,
    sum_send,
    sum_recv,
    hid_sem,
    d_sem,
):
    dp, tp = lax.axis_index("dp"), lax.axis_index("tp")
    z, core = lax.div(dp, 2), lax.rem(dp, 2)
    way = 1 - 2 * core
    tp_chip, tp_core = lax.div(tp, 2), lax.rem(tp, 2)
    owns = core == tp_core
    sibling = (dp + way, tp)

    def chip(steps):
        return lax.rem(z + way * steps + 2 * CHIPS, CHIPS)

    def along(steps):
        return (2 * chip(steps) + core, tp)

    def column(steps):
        return lax.rem(tp + steps, PLANE)

    def push(src, dst, send_sem, recv_sem, device):
        copy = pltpu.make_async_remote_copy(src, dst, send_sem, recv_sem, device, MESH)
        copy.start()
        return copy

    def landed(ref, sem):
        pltpu.make_async_remote_copy(ref, ref, sem, sem, sibling, MESH).wait_recv()

    def left(ref, sem):
        pltpu.make_async_remote_copy(ref, ref, sem, sem, sibling, MESH).wait_send()

    def others(ref, sem, wait):
        @pl.when(owns)
        def _():
            wait(ref.at[pl.ds(0, PLANE - 1)], sem)

        @pl.when(jnp.logical_not(owns))
        def _():
            wait(ref, sem)

    def load(src, dst, i):
        copy = pltpu.make_async_copy(src, dst, load_sem.at[i])
        copy.start()
        return copy

    load_q = load(queries.at[0], q_v, 0)
    load_k = load(cache.at[0], k_v, 1)
    load_small = [load(fresh, fresh_v, 2), load(residual, residual_v, 3), load(gain, gain_v, 4)]

    barrier = pltpu.get_barrier_semaphore()
    for i in range(1, PLANE):
        pl.semaphore_signal(barrier, inc=1, device_id=(dp, column(i)), device_id_type=MESH)
    for i in range(PLANE):
        pl.semaphore_signal(
            barrier, inc=1, device_id=(dp + way, column(i)), device_id_type=MESH
        )
    for i in range(1, CHIPS):
        pl.semaphore_signal(barrier, inc=1, device_id=along(i), device_id_type=MESH)

    gu_v[FEAT:PAD, :] = jnp.zeros((PAD - FEAT, WIDE), BF16)
    gu_v[PAD + FEAT :, :] = jnp.zeros((PAD - FEAT, WIDE), BF16)
    gu_v[:, 2 * UNITS :] = jnp.zeros((2 * PAD, WIDE - 2 * UNITS), BF16)
    row = lax.broadcasted_iota(jnp.int32, (16, 128), 0)
    ones = jnp.where(row < 2, 1.0, 0.0).astype(BF16)
    gu_v[FEAT : FEAT + 16, 2 * UNITS :] = ones
    gu_v[PAD + FEAT : PAD + FEAT + 16, 2 * UNITS :] = ones

    load_q.wait()
    load_k.wait()
    for h in range(OWN_HEADS):
        load(value_up.at[h], vu_v.at[:, pl.ds(128 * h, 128)], 5)
    mine = pl.ds(pl.multiple_of(core * PAD, PAD), FEAT)
    weights = [
        (out_weight, ow_v.at[core]),
        (gate_weight, gu_v.at[mine, pl.ds(0, UNITS)]),
        (up_weight, gu_v.at[mine, pl.ds(UNITS, UNITS)]),
        (down_weight, dw_v.at[core]),
    ]
    load_w = [load(src, dst, 6 + i) for i, (src, dst) in enumerate(weights)]
    q = q_v[...].T
    scores = jnp.dot(q, k_v[...], preferred_element_type=F32)
    for copy in load_small:
        copy.wait()
    position = lax.broadcasted_iota(jnp.int32, (HEADS, CACHE), 1)
    scores = jnp.where(position < length[0], scores * SCALE, -1e30)
    new = fresh_v[...].astype(F32)
    own = jnp.sum(q.astype(F32) * new, axis=1, keepdims=True) * SCALE
    top = jnp.maximum(own, jnp.max(scores, axis=1, keepdims=True))
    weight = jnp.exp(scores - top)
    own_weight = jnp.exp(own - top)
    total = jnp.sum(weight, axis=1, keepdims=True) + own_weight
    summed = by_columns(weight.astype(BF16), k_v[:LATENT, :])
    latent = ((summed + own_weight * new[:, :LATENT]) / total).reshape(PLANE, OWN_HEADS, LATENT)
    half = LATENT // 2
    head_out[...] = jnp.concatenate([latent[:, :, :half], latent[:, :, half:]], axis=1).astype(BF16)

    pl.semaphore_wait(barrier, 2 * PLANE - 1 + CHIPS - 1)
    for i in range(1, PLANE):
        to = column(i)
        push(head_out.at[to], head_in.at[tp], head_sem.at[0], head_sem.at[1], (dp, to))
    swaps = [
        push(src, dst, swap_send.at[i], swap_recv.at[i], sibling)
        for i, (src, dst) in enumerate(weights)
    ]
    head_in[tp] = head_out[tp]
    pltpu.make_async_copy(vu_v, vu_v, load_sem.at[5]).wait()
    landed(head_in.at[pl.ds(0, PLANE - 1)], head_sem.at[1])

    wide = head_in[...].astype(F32)
    latents = jnp.concatenate([wide[:, :OWN_HEADS], wide[:, OWN_HEADS:]], axis=2)
    latents = latents.reshape(PLANE * OWN_HEADS, LATENT).astype(BF16)
    products = jnp.dot(latents, vu_v[...], preferred_element_type=F32)
    row_head = lax.broadcasted_iota(jnp.int32, products.shape, 0) & (OWN_HEADS - 1)
    column_head = lax.broadcasted_iota(jnp.int32, products.shape, 1) >> 7
    products = jnp.where(row_head == column_head, products, 0.0).astype(BF16)
    to_row = lax.broadcasted_iota(jnp.int32, (ROWS, PLANE * OWN_HEADS), 0)
    from_row = lax.broadcasted_iota(jnp.int32, (ROWS, PLANE * OWN_HEADS), 1) >> 3
    pick = jnp.where(to_row == from_row, 1.0, 0.0).astype(BF16)
    val[z] = jnp.dot(pick, products, preferred_element_type=F32).astype(BF16)

    def gather(buf, sem, use):
        for d in SEND_ORDER:
            group = [d in g for g in GROUPS].index(True)
            push(buf.at[z], buf.at[z], sem.at[0], sem.at[group], along(d))
        for n, group in enumerate(GROUPS):
            if n:
                landed(buf.at[pl.ds(0, len(group))], sem.at[n])
            use([chip(-d) for d in group])

    def gather_end(buf, sem):
        left(buf.at[pl.ds(0, CHIPS - 1)], sem.at[0])

    def project(buf, w, dst_out, dst_in, sem):
        def use(chips):
            rows = jnp.concatenate([buf[c] for c in chips], axis=0) if len(chips) > 1 else buf[chips[0]]
            for to in range(2):
                sums = by_columns(rows, w[to]).astype(BF16)
                for n, c in enumerate(chips):
                    dst_out[2 * c + to, :, :FEAT] = sums[n * ROWS : (n + 1) * ROWS]
            for c in chips:
                owner = 2 * c + core
                there = dst_out.at[2 * c + 1 - core]
                push(there, dst_in.at[tp], sem.at[0], sem.at[1], (dp + way, owner))

                @pl.when(owner != tp)
                def _():
                    push(dst_out.at[owner], dst_in.at[tp], sem.at[0], sem.at[1], (dp, owner))

                @pl.when(owner == tp)
                def _():
                    dst_in[tp] = dst_out[owner]

        return use

    def collect(dst_in, sem):
        others(dst_in, sem.at[1], landed)
        return jnp.sum(dst_in[...].astype(F32), axis=0)

    load_w[0].wait()
    swaps[0].wait_recv()
    gather(val, val_sem, project(val, ow_v, o_out, o_in, o_sem))
    attention = collect(o_in, o_sem)
    stream = residual_v[...].astype(F32) + attention[:, :FEAT]

    squares = jnp.sum(stream * stream, axis=1, keepdims=True)
    high = squares.astype(BF16).astype(F32)
    lane = lax.broadcasted_iota(jnp.int32, (ROWS, PAD - FEAT), 1)
    extra = jnp.where(lane == 0, high, jnp.where(lane == 1, squares - high, 0.0))
    x_out[:, :FEAT] = (stream * gain_v[...]).astype(BF16)
    x_out[:, FEAT:] = extra.astype(BF16)
    slot = 2 * tp_chip + core
    for i in range(1, PLANE):
        push(x_out, x_in.at[slot], x_sem.at[0], x_sem.at[1], (2 * z + tp_core, column(i)))

    @pl.when(jnp.logical_not(owns))
    def _():
        push(x_out, x_in.at[slot], x_sem.at[0], x_sem.at[1], sibling)

    @pl.when(owns)
    def _():
        x_in[slot] = x_out[...]

    for copy in load_w[1:3]:
        copy.wait()
    for copy in swaps[1:3]:
        copy.wait_recv()
    others(x_in, x_sem.at[1], landed)

    def rows_for(steps):
        blocks = [
            jnp.concatenate([x_in[2 * chip(d)], x_in[2 * chip(d) + 1]], axis=1) for d in steps
        ]
        return jnp.concatenate(blocks, axis=0)

    def onward(value, i, n, device, group):
        lo, size = CUTS[n]
        cut = pl.ds(lo, size)
        sum_out[i, :, lo : lo + size] = value.astype(BF16)
        push(
            sum_out.at[i, :, cut],
            sum_in.at[i, :, cut],
            sum_send.at[n],
            sum_recv.at[n, group],
            along(device),
        )

    def came(first, count, n, group):
        lo, size = CUTS[n]
        landed(sum_in.at[pl.ds(first, count), :, pl.ds(lo, size)], sum_recv.at[n, group])
        return [sum_in[first + k, :, lo : lo + size].astype(F32) for k in range(count)]

    far, near = rows_for((4, 3, -3)), rows_for((1, -1, 2, -2, 0))
    for n, (lo, size) in enumerate(CUTS):
        sums = jnp.dot(far, gu_v[:, lo : lo + size], preferred_element_type=F32)
        onward(sums[:ROWS], 0, n, 2, 0)
        onward(sums[ROWS : 2 * ROWS], 1, n, 1, 0)
        onward(sums[2 * ROWS :], 2, n, -1, 1)
    for n, (lo, size) in enumerate(CUTS):
        sums = jnp.dot(near, gu_v[:, lo : lo + size], preferred_element_type=F32)
        onward(sums[:ROWS], 3, n, 1, 2)
        onward(sums[ROWS : 2 * ROWS], 4, n, -1, 2)
        part[:, lo : lo + size] = sums[2 * ROWS :]
    for n, (lo, size) in enumerate(CUTS):
        a, b = came(0, 2, n, 0)
        onward(part[:ROWS, lo : lo + size] + a + b, 5, n, 2, 2)
        (a,) = came(2, 1, n, 1)
        onward(part[ROWS : 2 * ROWS, lo : lo + size] + a, 6, n, -2, 2)
    whole = []
    for n, (lo, size) in enumerate(CUTS):
        a, b, c, d = came(3, 4, n, 2)
        whole.append(part[2 * ROWS :, lo : lo + size] + (a + b) + (c + d))
    whole = jnp.concatenate(whole, axis=1)
    inverse = lax.rsqrt(whole[:, 2 * UNITS : 2 * UNITS + 1] * (1.0 / D) + 1e-06)
    gate = whole[:, :UNITS] * inverse
    up = whole[:, UNITS : 2 * UNITS] * inverse
    hid[z] = (gate / (1.0 + jnp.exp(-gate)) * up).astype(BF16)

    load_w[3].wait()
    swaps[3].wait_recv()
    gather(hid, hid_sem, project(hid, dw_v, d_out, d_in, d_sem))
    lowered = collect(d_in, d_sem)
    out[...] = (stream + lowered[:, :FEAT]).astype(BF16)

    for copy in swaps:
        copy.wait_send()
    left(head_out.at[pl.ds(0, PLANE - 1)], head_sem.at[0])
    gather_end(val, val_sem)
    others(o_out, o_sem.at[0], left)
    others(x_in, x_sem.at[0], left)
    for n, (lo, size) in enumerate(CUTS):
        left(sum_out.at[:, :, pl.ds(lo, size)], sum_send.at[n])
    gather_end(hid, hid_sem)
    others(d_out, d_sem.at[0], left)


def layer(
    queries,
    new_latent,
    latent_cache,
    cached_lengths,
    value_up,
    out_weight,
    residual_in,
    norm_gain,
    gate_weight,
    up_weight,
    down_weight,
):
    anywhere = pl.BlockSpec(memory_space=pl.ANY)
    smem = pl.BlockSpec(memory_space=pltpu.SMEM)
    dma = pltpu.SemaphoreType.DMA
    return pl.pallas_call(
        kernel,
        out_shape=jax.ShapeDtypeStruct((ROWS, FEAT), BF16),
        in_specs=[anywhere] * 3 + [smem] + [anywhere] * 7,
        out_specs=pl.BlockSpec(memory_space=pltpu.VMEM),
        scratch_shapes=[
            pltpu.VMEM((KEY, HEADS), BF16),
            pltpu.VMEM((KEY, CACHE), BF16),
            pltpu.VMEM((1, KEY), BF16),
            pltpu.VMEM((ROWS, FEAT), BF16),
            pltpu.VMEM((1, FEAT), F32),
            pltpu.VMEM((LATENT, VALUES), BF16),
            pltpu.VMEM((2, FEAT, VALUES), BF16),
            pltpu.VMEM((2 * PAD, WIDE), BF16),
            pltpu.VMEM((2, FEAT, UNITS), BF16),
            pltpu.VMEM((PLANE, ROWS, LATENT // 2), BF16),
            pltpu.VMEM((PLANE, ROWS, LATENT // 2), BF16),
            pltpu.VMEM((CHIPS, ROWS, VALUES), BF16),
            pltpu.VMEM((PLANE, ROWS, PAD), BF16),
            pltpu.VMEM((PLANE, ROWS, PAD), BF16),
            pltpu.VMEM((ROWS, PAD), BF16),
            pltpu.VMEM((PLANE, ROWS, PAD), BF16),
            pltpu.VMEM((3 * ROWS, WIDE), F32),
            pltpu.VMEM((7, ROWS, WIDE), BF16),
            pltpu.VMEM((7, ROWS, WIDE), BF16),
            pltpu.VMEM((CHIPS, ROWS, UNITS), BF16),
            pltpu.VMEM((PLANE, ROWS, PAD), BF16),
            pltpu.VMEM((PLANE, ROWS, PAD), BF16),
            dma((10,)),
            dma((4,)),
            dma((4,)),
            dma((2,)),
            dma((len(GROUPS),)),
            dma((2,)),
            dma((2,)),
            dma((len(CUTS),)),
            dma((len(CUTS), 3)),
            dma((len(GROUPS),)),
            dma((2,)),
        ],
        compiler_params=pltpu.CompilerParams(
            collective_id=0, has_side_effects=True, vmem_limit_bytes=60 * 1024 * 1024
        ),
    )(
        queries.transpose(0, 2, 1),
        new_latent,
        latent_cache.transpose(0, 2, 1),
        cached_lengths,
        value_up,
        out_weight.T,
        residual_in,
        norm_gain.reshape(1, FEAT),
        gate_weight,
        up_weight,
        down_weight.T,
    )


def solution(mesh):
    in_specs = (
        P(("dp", "tp"), None, None),
        P(("dp", "tp"), None),
        P(("dp", "tp"), None, None),
        P(("dp", "tp")),
        P("tp", None, None),
        P("tp", "dp"),
        P("tp", "dp"),
        P("dp"),
        P("dp", "tp"),
        P("dp", "tp"),
        P("tp", "dp"),
    )
    return jax.shard_map(
        layer, mesh=mesh, in_specs=in_specs, out_specs=P("tp", "dp"), check_vma=False
    )
```

```python
import jax
import jax.numpy as jnp
from jax import lax
from jax.experimental import pallas as pl
from jax.experimental.pallas import tpu as pltpu
from jax.sharding import PartitionSpec as P

D = 7168
HEADS = 128
LATENT = 512
KEY = 576
CACHE = 1024
SCALE = (128 + 64) ** (-0.5)
PLANE = 16
CHIPS = 8
ROWS = 16
OWN_HEADS = 8
VALUES = 1024
FEAT = 448
PAD = 512
UNITS = 1152
WIDE = 2 * UNITS + 128
F32 = jnp.float32
BF16 = jnp.bfloat16
MESH = pl.DeviceIdType.MESH
FAR_FIRST = (10, 6, 9, 11, 14, 5, 7, 13, 15, 2, 8, 1, 3, 4, 12)
SEND_ORDER = (1, 7, 4, 2, 6, 3, 5)
GROUPS = ((0,), (1, 7), (2, 6, 4), (3, 5))
CUTS = ((0, 768), (768, 768), (1536, WIDE - 1536))


def by_columns(a, b):
    return lax.dot_general(a, b, (((1,), (1,)), ((), ())), preferred_element_type=F32)


def kernel(
    queries,
    fresh,
    cache,
    length,
    value_up,
    out_weight,
    residual,
    gain,
    gate_weight,
    up_weight,
    down_weight,
    out,
    q_v,
    k_v,
    length_s,
    fresh_v,
    residual_v,
    gain_v,
    vu_v,
    ow_v,
    gu_v,
    dw_v,
    head_out,
    head_in,
    val,
    o_out,
    o_in,
    x_out,
    x_in,
    part,
    sum_out,
    sum_in,
    hid,
    d_out,
    d_in,
    load_sem,
    swap_send,
    swap_recv,
    head_sem,
    val_sem,
    o_sem,
    x_sem,
    sum_send,
    sum_recv,
    hid_sem,
    d_sem,
):
    dp, tp = lax.axis_index("dp"), lax.axis_index("tp")
    z, core = lax.div(dp, 2), lax.rem(dp, 2)
    way = 1 - 2 * core
    tp_chip, tp_core = lax.div(tp, 2), lax.rem(tp, 2)
    owns = core == tp_core
    owns_later = core != tp_core
    sibling = (dp + way, tp)
    spin = 1 + 2 * lax.rem(tp + lax.div(tp, 4), 2)

    def chip(steps):
        return lax.rem(z + way * steps + 4 * CHIPS, CHIPS)

    def along(steps):
        return (2 * chip(steps) + core, tp)

    def column(steps):
        return lax.rem(tp + steps, PLANE)


    def push(src, dst, send_sem, recv_sem, device):
        copy = pltpu.make_async_remote_copy(src, dst, send_sem, recv_sem, device, MESH)
        copy.start()
        return copy

    def landed(ref, sem):
        pltpu.make_async_remote_copy(ref, ref, sem, sem, sibling, MESH).wait_recv()

    def left(ref, sem):
        pltpu.make_async_remote_copy(ref, ref, sem, sem, sibling, MESH).wait_send()

    def others(ref, sem, wait, owned):
        @pl.when(owned)
        def _():
            wait(ref.at[pl.ds(0, PLANE - 1)], sem)

        @pl.when(jnp.logical_not(owned))
        def _():
            wait(ref, sem)

    def load(src, dst, i):
        copy = pltpu.make_async_copy(src, dst, load_sem.at[i])
        copy.start()
        return copy

    load_q = load(queries.at[0], q_v, 0)
    load_k = load(cache.at[0], k_v, 1)
    load_small = [
        load(fresh, fresh_v, 2),
        load(residual, residual_v, 3),
        load(gain, gain_v, 4),
        load(length, length_s, 10),
    ]

    barrier = pltpu.get_barrier_semaphore()
    for i in FAR_FIRST:
        pl.semaphore_signal(barrier, inc=1, device_id=(dp, column(i)), device_id_type=MESH)
    for i in range(PLANE):
        pl.semaphore_signal(
            barrier, inc=1, device_id=(dp + way, column(i)), device_id_type=MESH
        )
    for i in range(1, CHIPS):
        pl.semaphore_signal(barrier, inc=1, device_id=along(i), device_id_type=MESH)

    gu_v[FEAT:PAD, :] = jnp.zeros((PAD - FEAT, WIDE), BF16)
    gu_v[PAD + FEAT :, :] = jnp.zeros((PAD - FEAT, WIDE), BF16)
    gu_v[:, 2 * UNITS :] = jnp.zeros((2 * PAD, WIDE - 2 * UNITS), BF16)
    row = lax.broadcasted_iota(jnp.int32, (16, 128), 0)
    ones = jnp.where(row < 2, 1.0, 0.0).astype(BF16)
    gu_v[FEAT : FEAT + 16, 2 * UNITS :] = ones
    gu_v[PAD + FEAT : PAD + FEAT + 16, 2 * UNITS :] = ones

    load_q.wait()
    load_k.wait()
    for h in range(OWN_HEADS):
        load(value_up.at[h], vu_v.at[:, pl.ds(128 * h, 128)], 5)
    mine = pl.ds(pl.multiple_of(core * PAD, PAD), FEAT)
    weights = [
        (out_weight, ow_v.at[core]),
        (gate_weight, gu_v.at[mine, pl.ds(0, UNITS)]),
        (up_weight, gu_v.at[mine, pl.ds(UNITS, UNITS)]),
        (down_weight, dw_v.at[core]),
    ]
    load_w = [load(src, dst, 6 + i) for i, (src, dst) in enumerate(weights)]
    q = q_v[...].T
    scores = jnp.dot(q, k_v[...], preferred_element_type=F32)
    for copy in load_small:
        copy.wait()
    position = lax.broadcasted_iota(jnp.int32, (HEADS, CACHE), 1)
    scores = jnp.where(position < length_s[0], scores * SCALE, -1e30)
    new = fresh_v[...].astype(F32)
    own = jnp.sum(q.astype(F32) * new, axis=1, keepdims=True) * SCALE
    top = jnp.maximum(own, jnp.max(scores, axis=1, keepdims=True))
    weight = jnp.exp(scores - top)
    own_weight = jnp.exp(own - top)
    total = jnp.sum(weight, axis=1, keepdims=True) + own_weight
    summed = by_columns(weight.astype(BF16), k_v[:LATENT, :])
    latent = ((summed + own_weight * new[:, :LATENT]) / total).reshape(PLANE, OWN_HEADS, LATENT)
    half = LATENT // 2
    head_out[...] = jnp.concatenate([latent[:, :, :half], latent[:, :, half:]], axis=1).astype(BF16)

    pl.semaphore_wait(barrier, 2 * PLANE - 1 + CHIPS - 1)
    for i in FAR_FIRST:
        to = column(i)
        push(head_out.at[to], head_in.at[tp], head_sem.at[0], head_sem.at[1], (dp, to))
    swaps = [
        push(src, dst, swap_send.at[i], swap_recv.at[i], sibling)
        for i, (src, dst) in enumerate(weights)
    ]
    head_in[tp] = head_out[tp]
    pltpu.make_async_copy(vu_v, vu_v, load_sem.at[5]).wait()
    landed(head_in.at[pl.ds(0, PLANE - 1)], head_sem.at[1])

    wide = head_in[...].astype(F32)
    latents = jnp.concatenate([wide[:, :OWN_HEADS], wide[:, OWN_HEADS:]], axis=2)
    latents = latents.reshape(PLANE * OWN_HEADS, LATENT).astype(BF16)
    products = jnp.dot(latents, vu_v[...], preferred_element_type=F32)
    row_head = lax.broadcasted_iota(jnp.int32, products.shape, 0) & (OWN_HEADS - 1)
    column_head = lax.broadcasted_iota(jnp.int32, products.shape, 1) >> 7
    products = jnp.where(row_head == column_head, products, 0.0).astype(BF16)
    to_row = lax.broadcasted_iota(jnp.int32, (ROWS, PLANE * OWN_HEADS), 0)
    from_row = lax.broadcasted_iota(jnp.int32, (ROWS, PLANE * OWN_HEADS), 1) >> 3
    pick = jnp.where(to_row == from_row, 1.0, 0.0).astype(BF16)
    val[z] = jnp.dot(pick, products, preferred_element_type=F32).astype(BF16)

    def gather(buf, sem, use):
        for d in SEND_ORDER:
            group = [d in g for g in GROUPS].index(True)
            push(buf.at[z], buf.at[z], sem.at[0], sem.at[group], along(spin * d))
        for n, group in enumerate(GROUPS):
            if n:
                landed(buf.at[pl.ds(0, len(group))], sem.at[n])
            use([chip(-spin * d) for d in group])

    def gather_end(buf, sem):
        left(buf.at[pl.ds(0, CHIPS - 1)], sem.at[0])

    def project(buf, w, dst_out, dst_in, sem, parity):
        def use(chips):
            rows = jnp.concatenate([buf[c] for c in chips], axis=0) if len(chips) > 1 else buf[chips[0]]
            for to in range(2):
                sums = by_columns(rows, w[to]).astype(BF16)
                for n, c in enumerate(chips):
                    dst_out[2 * c + to, :, :FEAT] = sums[n * ROWS : (n + 1) * ROWS]
            for c in chips:
                owner = 2 * c + parity
                here = dst_out.at[2 * c + core]
                there = dst_out.at[2 * c + 1 - core]
                push(there, dst_in.at[tp], sem.at[0], sem.at[1], (dp + way, owner))

                @pl.when(owner != tp)
                def _():
                    push(here, dst_in.at[tp], sem.at[0], sem.at[1], (dp, owner))

                @pl.when(owner == tp)
                def _():
                    dst_in[tp] = here[...]

        return use

    def collect(dst_in, sem, owned):
        others(dst_in, sem.at[1], landed, owned)
        return jnp.sum(dst_in[...].astype(F32), axis=0)

    load_w[0].wait()
    swaps[0].wait_recv()
    gather(val, val_sem, project(val, ow_v, o_out, o_in, o_sem, core))
    attention = collect(o_in, o_sem, owns)
    stream = residual_v[...].astype(F32) + attention[:, :FEAT]

    squares = jnp.sum(stream * stream, axis=1, keepdims=True)
    high = squares.astype(BF16).astype(F32)
    lane = lax.broadcasted_iota(jnp.int32, (ROWS, PAD - FEAT), 1)
    extra = jnp.where(lane == 0, high, jnp.where(lane == 1, squares - high, 0.0))
    x_out[:, :FEAT] = (stream * gain_v[...]).astype(BF16)
    x_out[:, FEAT:] = extra.astype(BF16)
    slot = 2 * tp_chip + core
    for i in FAR_FIRST:
        push(x_out, x_in.at[slot], x_sem.at[0], x_sem.at[1], (2 * z + 1 - tp_core, column(i)))

    @pl.when(owns)
    def _():
        push(x_out, x_in.at[slot], x_sem.at[0], x_sem.at[1], sibling)

    @pl.when(owns_later)
    def _():
        x_in[slot] = x_out[...]

    for copy in load_w[1:3]:
        copy.wait()
    for copy in swaps[1:3]:
        copy.wait_recv()
    others(x_in, x_sem.at[1], landed, owns_later)

    def rows_for(steps):
        blocks = [
            jnp.concatenate([x_in[2 * chip(d)], x_in[2 * chip(d) + 1]], axis=1) for d in steps
        ]
        return jnp.concatenate(blocks, axis=0)

    def onward(value, i, n, device, group):
        lo, size = CUTS[n]
        cut = pl.ds(lo, size)
        sum_out[i, :, lo : lo + size] = value.astype(BF16)
        push(
            sum_out.at[i, :, cut],
            sum_in.at[i, :, cut],
            sum_send.at[n],
            sum_recv.at[n, group],
            along(device),
        )

    def came(first, count, n, group):
        lo, size = CUTS[n]
        landed(sum_in.at[pl.ds(first, count), :, pl.ds(lo, size)], sum_recv.at[n, group])
        return [sum_in[first + k, :, lo : lo + size].astype(F32) for k in range(count)]

    far, near = rows_for((4, 3, -3)), rows_for((1, -1, 2, -2, 0))
    for n, (lo, size) in enumerate(CUTS):
        sums = jnp.dot(far, gu_v[:, lo : lo + size], preferred_element_type=F32)
        onward(sums[:ROWS], 0, n, 2, 0)
        onward(sums[ROWS : 2 * ROWS], 1, n, 1, 0)
        onward(sums[2 * ROWS :], 2, n, -1, 1)
    for n, (lo, size) in enumerate(CUTS):
        sums = jnp.dot(near, gu_v[:, lo : lo + size], preferred_element_type=F32)
        onward(sums[:ROWS], 3, n, 1, 2)
        onward(sums[ROWS : 2 * ROWS], 4, n, -1, 2)
        part[:, lo : lo + size] = sums[2 * ROWS :]
    for n, (lo, size) in enumerate(CUTS):
        a, b = came(0, 2, n, 0)
        onward(part[:ROWS, lo : lo + size] + a + b, 5, n, 2, 2)
        (a,) = came(2, 1, n, 1)
        onward(part[ROWS : 2 * ROWS, lo : lo + size] + a, 6, n, -2, 2)
    whole = []
    for n, (lo, size) in enumerate(CUTS):
        a, b, c, d = came(3, 4, n, 2)
        whole.append(part[2 * ROWS :, lo : lo + size] + (a + b) + (c + d))
    whole = jnp.concatenate(whole, axis=1)
    inverse = lax.rsqrt(whole[:, 2 * UNITS : 2 * UNITS + 1] * (1.0 / D) + 1e-06)
    gate = whole[:, :UNITS] * inverse
    up = whole[:, UNITS : 2 * UNITS] * inverse
    hid[z] = (gate / (1.0 + jnp.exp(-gate)) * up).astype(BF16)

    load_w[3].wait()
    swaps[3].wait_recv()
    gather(hid, hid_sem, project(hid, dw_v, d_out, d_in, d_sem, 1 - core))
    lowered = collect(d_in, d_sem, owns_later)
    out[...] = (stream + lowered[:, :FEAT]).astype(BF16)

    for copy in swaps:
        copy.wait_send()
    left(head_out.at[pl.ds(0, PLANE - 1)], head_sem.at[0])
    gather_end(val, val_sem)
    others(o_out, o_sem.at[0], left, owns)
    others(x_in, x_sem.at[0], left, owns_later)
    for n, (lo, size) in enumerate(CUTS):
        left(sum_out.at[:, :, pl.ds(lo, size)], sum_send.at[n])
    gather_end(hid, hid_sem)
    others(d_out, d_sem.at[0], left, owns_later)


def layer(
    queries,
    new_latent,
    latent_cache,
    cached_lengths,
    value_up,
    out_weight,
    residual_in,
    norm_gain,
    gate_weight,
    up_weight,
    down_weight,
):
    anywhere = pl.BlockSpec(memory_space=pl.ANY)
    dma = pltpu.SemaphoreType.DMA
    return pl.pallas_call(
        kernel,
        out_shape=jax.ShapeDtypeStruct((ROWS, FEAT), BF16),
        in_specs=[anywhere] * 11,
        out_specs=pl.BlockSpec(memory_space=pltpu.VMEM),
        scratch_shapes=[
            pltpu.VMEM((KEY, HEADS), BF16),
            pltpu.VMEM((KEY, CACHE), BF16),
            pltpu.SMEM((1,), jnp.int32),
            pltpu.VMEM((1, KEY), BF16),
            pltpu.VMEM((ROWS, FEAT), BF16),
            pltpu.VMEM((1, FEAT), F32),
            pltpu.VMEM((LATENT, VALUES), BF16),
            pltpu.VMEM((2, FEAT, VALUES), BF16),
            pltpu.VMEM((2 * PAD, WIDE), BF16),
            pltpu.VMEM((2, FEAT, UNITS), BF16),
            pltpu.VMEM((PLANE, ROWS, LATENT // 2), BF16),
            pltpu.VMEM((PLANE, ROWS, LATENT // 2), BF16),
            pltpu.VMEM((CHIPS, ROWS, VALUES), BF16),
            pltpu.VMEM((PLANE, ROWS, PAD), BF16),
            pltpu.VMEM((PLANE, ROWS, PAD), BF16),
            pltpu.VMEM((ROWS, PAD), BF16),
            pltpu.VMEM((PLANE, ROWS, PAD), BF16),
            pltpu.VMEM((3 * ROWS, WIDE), F32),
            pltpu.VMEM((7, ROWS, WIDE), BF16),
            pltpu.VMEM((7, ROWS, WIDE), BF16),
            pltpu.VMEM((CHIPS, ROWS, UNITS), BF16),
            pltpu.VMEM((PLANE, ROWS, PAD), BF16),
            pltpu.VMEM((PLANE, ROWS, PAD), BF16),
            dma((11,)),
            dma((4,)),
            dma((4,)),
            dma((2,)),
            dma((len(GROUPS),)),
            dma((2,)),
            dma((2,)),
            dma((len(CUTS),)),
            dma((len(CUTS), 3)),
            dma((len(GROUPS),)),
            dma((2,)),
        ],
        compiler_params=pltpu.CompilerParams(
            collective_id=0, has_side_effects=True, vmem_limit_bytes=60 * 1024 * 1024
        ),
    )(
        queries.transpose(0, 2, 1),
        new_latent,
        latent_cache.transpose(0, 2, 1),
        cached_lengths,
        value_up,
        out_weight.T,
        residual_in,
        norm_gain.reshape(1, FEAT),
        gate_weight,
        up_weight,
        down_weight.T,
    )


def solution(mesh):
    in_specs = (
        P(("dp", "tp"), None, None),
        P(("dp", "tp"), None),
        P(("dp", "tp"), None, None),
        P(("dp", "tp")),
        P("tp", None, None),
        P("tp", "dp"),
        P("tp", "dp"),
        P("dp"),
        P("dp", "tp"),
        P("dp", "tp"),
        P("tp", "dp"),
    )
    return jax.shard_map(
        layer, mesh=mesh, in_specs=in_specs, out_specs=P("tp", "dp"), check_vma=False
    )
```

```python
import jax
import jax.numpy as jnp
from jax import lax
from jax.experimental import pallas as pl
from jax.experimental.pallas import tpu as pltpu
from jax.sharding import PartitionSpec as P

D = 7168
HEADS = 128
LATENT = 512
KEY = 576
CACHE = 1024
SCALE = (128 + 64) ** (-0.5)
PLANE = 16
CHIPS = 8
ROWS = 16
OWN_HEADS = 8
VALUES = 1024
FEAT = 448
PAD = 512
UNITS = 1152
WIDE = 2 * UNITS + 128
F32 = jnp.float32
BF16 = jnp.bfloat16
MESH = pl.DeviceIdType.MESH
FAR_FIRST = (10, 6, 9, 11, 14, 5, 7, 13, 15, 2, 8, 1, 3, 4, 12)
VAL_PLAN = ((1, 7, 2, 6, 3, 5, 4), {}, ((0,), (1, 7), (2, 6), (3, 5, 4)))
HID_PLAN = ((2, 6, 1, 7), {2: (2, 1), 6: (-1,)}, ((0,), (2, 6), (1, 7), (3, 5, 4)))
CUTS = ((0, 768), (768, 768), (1536, WIDE - 1536))


def by_columns(a, b):
    return lax.dot_general(a, b, (((1,), (1,)), ((), ())), preferred_element_type=F32)


def kernel(
    queries,
    fresh,
    cache,
    length,
    value_up,
    out_weight,
    residual,
    gain,
    gate_weight,
    up_weight,
    down_weight,
    out,
    q_v,
    k_v,
    length_s,
    fresh_v,
    residual_v,
    gain_v,
    vu_v,
    ow_v,
    gu_v,
    dw_v,
    head_out,
    head_in,
    val,
    o_out,
    o_in,
    x_out,
    x_in,
    part,
    sum_out,
    sum_in,
    hid,
    d_out,
    d_in,
    load_sem,
    swap_send,
    swap_recv,
    head_sem,
    val_sem,
    o_sem,
    x_sem,
    sum_send,
    sum_recv,
    hid_sem,
    d_sem,
):
    dp, tp = lax.axis_index("dp"), lax.axis_index("tp")
    z, core = lax.div(dp, 2), lax.rem(dp, 2)
    way = 1 - 2 * core
    tp_chip, tp_core = lax.div(tp, 2), lax.rem(tp, 2)
    owns = core == tp_core
    owns_later = core != tp_core
    sibling = (dp + way, tp)

    def chip(steps):
        return lax.rem(z + way * steps + 2 * CHIPS, CHIPS)

    def along(steps):
        return (2 * chip(steps) + core, tp)

    def column(steps):
        return lax.rem(tp + steps, PLANE)


    def push(src, dst, send_sem, recv_sem, device):
        copy = pltpu.make_async_remote_copy(src, dst, send_sem, recv_sem, device, MESH)
        copy.start()
        return copy

    def landed(ref, sem):
        pltpu.make_async_remote_copy(ref, ref, sem, sem, sibling, MESH).wait_recv()

    def left(ref, sem):
        pltpu.make_async_remote_copy(ref, ref, sem, sem, sibling, MESH).wait_send()

    def others(ref, sem, wait, owned):
        @pl.when(owned)
        def _():
            wait(ref.at[pl.ds(0, PLANE - 1)], sem)

        @pl.when(jnp.logical_not(owned))
        def _():
            wait(ref, sem)

    def load(src, dst, i):
        copy = pltpu.make_async_copy(src, dst, load_sem.at[i])
        copy.start()
        return copy

    load_q = load(queries.at[0], q_v, 0)
    load_k = load(cache.at[0], k_v, 1)
    load_small = [
        load(fresh, fresh_v, 2),
        load(residual, residual_v, 3),
        load(gain, gain_v, 4),
        load(length, length_s, 10),
    ]

    barrier = pltpu.get_barrier_semaphore()
    for i in FAR_FIRST:
        pl.semaphore_signal(barrier, inc=1, device_id=(dp, column(i)), device_id_type=MESH)
    for i in range(PLANE):
        pl.semaphore_signal(
            barrier, inc=1, device_id=(dp + way, column(i)), device_id_type=MESH
        )
    for i in range(1, CHIPS):
        pl.semaphore_signal(barrier, inc=1, device_id=along(i), device_id_type=MESH)

    gu_v[FEAT:PAD, :] = jnp.zeros((PAD - FEAT, WIDE), BF16)
    gu_v[PAD + FEAT :, :] = jnp.zeros((PAD - FEAT, WIDE), BF16)
    gu_v[:, 2 * UNITS :] = jnp.zeros((2 * PAD, WIDE - 2 * UNITS), BF16)
    row = lax.broadcasted_iota(jnp.int32, (16, 128), 0)
    ones = jnp.where(row < 2, 1.0, 0.0).astype(BF16)
    gu_v[FEAT : FEAT + 16, 2 * UNITS :] = ones
    gu_v[PAD + FEAT : PAD + FEAT + 16, 2 * UNITS :] = ones

    load_q.wait()
    load_k.wait()
    for h in range(OWN_HEADS):
        load(value_up.at[h], vu_v.at[:, pl.ds(128 * h, 128)], 5)
    mine = pl.ds(pl.multiple_of(core * PAD, PAD), FEAT)
    weights = [
        (out_weight, ow_v.at[core]),
        (gate_weight, gu_v.at[mine, pl.ds(0, UNITS)]),
        (up_weight, gu_v.at[mine, pl.ds(UNITS, UNITS)]),
        (down_weight, dw_v.at[core]),
    ]
    load_w = [load(src, dst, 6 + i) for i, (src, dst) in enumerate(weights)]
    q = q_v[...].T
    scores = jnp.dot(q, k_v[...], preferred_element_type=F32)
    for copy in load_small:
        copy.wait()
    position = lax.broadcasted_iota(jnp.int32, (HEADS, CACHE), 1)
    scores = jnp.where(position < length_s[0], scores * SCALE, -1e30)
    new = fresh_v[...].astype(F32)
    own = jnp.sum(q.astype(F32) * new, axis=1, keepdims=True) * SCALE
    top = jnp.maximum(own, jnp.max(scores, axis=1, keepdims=True))
    weight = jnp.exp(scores - top)
    own_weight = jnp.exp(own - top)
    total = jnp.sum(weight, axis=1, keepdims=True) + own_weight
    summed = by_columns(weight.astype(BF16), k_v[:LATENT, :])
    latent = ((summed + own_weight * new[:, :LATENT]) / total).reshape(PLANE, OWN_HEADS, LATENT)
    half = LATENT // 2
    head_out[...] = jnp.concatenate([latent[:, :, :half], latent[:, :, half:]], axis=1).astype(BF16)

    pl.semaphore_wait(barrier, 2 * PLANE - 1 + CHIPS - 1)
    for i in FAR_FIRST:
        to = column(i)
        push(head_out.at[to], head_in.at[tp], head_sem.at[0], head_sem.at[1], (dp, to))
    swaps = [
        push(src, dst, swap_send.at[i], swap_recv.at[i], sibling)
        for i, (src, dst) in enumerate(weights)
    ]
    head_in[tp] = head_out[tp]
    pltpu.make_async_copy(vu_v, vu_v, load_sem.at[5]).wait()
    landed(head_in.at[pl.ds(0, PLANE - 1)], head_sem.at[1])

    wide = head_in[...].astype(F32)
    latents = jnp.concatenate([wide[:, :OWN_HEADS], wide[:, OWN_HEADS:]], axis=2)
    latents = latents.reshape(PLANE * OWN_HEADS, LATENT).astype(BF16)
    products = jnp.dot(latents, vu_v[...], preferred_element_type=F32)
    row_head = lax.broadcasted_iota(jnp.int32, products.shape, 0) & (OWN_HEADS - 1)
    column_head = lax.broadcasted_iota(jnp.int32, products.shape, 1) >> 7
    products = jnp.where(row_head == column_head, products, 0.0).astype(BF16)
    to_row = lax.broadcasted_iota(jnp.int32, (ROWS, PLANE * OWN_HEADS), 0)
    from_row = lax.broadcasted_iota(jnp.int32, (ROWS, PLANE * OWN_HEADS), 1) >> 3
    pick = jnp.where(to_row == from_row, 1.0, 0.0).astype(BF16)
    val[z] = jnp.dot(pick, products, preferred_element_type=F32).astype(BF16)

    def gather(buf, sem, use, order, relays, groups):
        def group_of(d):
            return [d % CHIPS in g for g in groups].index(True)

        for d in order:
            push(buf.at[z], buf.at[z], sem.at[0], sem.at[group_of(d)], along(d))
        for n, group in enumerate(groups):
            if n:
                landed(buf.at[pl.ds(0, len(group))], sem.at[n])
            for d in group:
                for step in relays.get(d, ()):
                    block = buf.at[chip(-d)]
                    push(block, block, sem.at[0], sem.at[group_of(d + step)], along(step))
            use([chip(-d) for d in group])

    def gather_end(buf, sem):
        left(buf.at[pl.ds(0, CHIPS - 1)], sem.at[0])

    def project(buf, w, dst_out, dst_in, sem, parity):
        def use(chips):
            rows = jnp.concatenate([buf[c] for c in chips], axis=0) if len(chips) > 1 else buf[chips[0]]
            for to in range(2):
                sums = by_columns(rows, w[to]).astype(BF16)
                for n, c in enumerate(chips):
                    dst_out[2 * c + to, :, :FEAT] = sums[n * ROWS : (n + 1) * ROWS]
            for c in chips:
                owner = 2 * c + parity
                here = dst_out.at[2 * c + core]
                there = dst_out.at[2 * c + 1 - core]
                push(there, dst_in.at[tp], sem.at[0], sem.at[1], (dp + way, owner))

                @pl.when(owner != tp)
                def _():
                    push(here, dst_in.at[tp], sem.at[0], sem.at[1], (dp, owner))

                @pl.when(owner == tp)
                def _():
                    dst_in[tp] = here[...]

        return use

    def collect(dst_in, sem, owned):
        others(dst_in, sem.at[1], landed, owned)
        return jnp.sum(dst_in[...].astype(F32), axis=0)

    load_w[0].wait()
    swaps[0].wait_recv()
    gather(val, val_sem, project(val, ow_v, o_out, o_in, o_sem, core), *VAL_PLAN)
    attention = collect(o_in, o_sem, owns)
    stream = residual_v[...].astype(F32) + attention[:, :FEAT]

    squares = jnp.sum(stream * stream, axis=1, keepdims=True)
    high = squares.astype(BF16).astype(F32)
    lane = lax.broadcasted_iota(jnp.int32, (ROWS, PAD - FEAT), 1)
    extra = jnp.where(lane == 0, high, jnp.where(lane == 1, squares - high, 0.0))
    x_out[:, :FEAT] = (stream * gain_v[...]).astype(BF16)
    x_out[:, FEAT:] = extra.astype(BF16)
    slot = 2 * tp_chip + core
    for i in FAR_FIRST:
        push(x_out, x_in.at[slot], x_sem.at[0], x_sem.at[1], (2 * z + 1 - tp_core, column(i)))

    @pl.when(owns)
    def _():
        push(x_out, x_in.at[slot], x_sem.at[0], x_sem.at[1], sibling)

    @pl.when(owns_later)
    def _():
        x_in[slot] = x_out[...]

    for copy in load_w[1:3]:
        copy.wait()
    for copy in swaps[1:3]:
        copy.wait_recv()
    others(x_in, x_sem.at[1], landed, owns_later)

    def rows_for(steps):
        blocks = [
            jnp.concatenate([x_in[2 * chip(d)], x_in[2 * chip(d) + 1]], axis=1) for d in steps
        ]
        return jnp.concatenate(blocks, axis=0)

    def onward(value, i, n, device, group):
        lo, size = CUTS[n]
        cut = pl.ds(lo, size)
        sum_out[i, :, lo : lo + size] = value.astype(BF16)
        push(
            sum_out.at[i, :, cut],
            sum_in.at[i, :, cut],
            sum_send.at[n],
            sum_recv.at[n, group],
            along(device),
        )

    def came(first, count, n, group):
        lo, size = CUTS[n]
        landed(sum_in.at[pl.ds(first, count), :, pl.ds(lo, size)], sum_recv.at[n, group])
        return [sum_in[first + k, :, lo : lo + size].astype(F32) for k in range(count)]

    far, near = rows_for((4, 3, -3)), rows_for((1, -1, 2, -2, 0))
    for n, (lo, size) in enumerate(CUTS):
        sums = jnp.dot(far, gu_v[:, lo : lo + size], preferred_element_type=F32)
        onward(sums[:ROWS], 0, n, 2, 0)
        onward(sums[ROWS : 2 * ROWS], 1, n, 1, 0)
        onward(sums[2 * ROWS :], 2, n, -1, 1)
    for n, (lo, size) in enumerate(CUTS):
        sums = jnp.dot(near, gu_v[:, lo : lo + size], preferred_element_type=F32)
        onward(sums[:ROWS], 3, n, 1, 2)
        onward(sums[ROWS : 2 * ROWS], 4, n, -1, 2)
        part[:, lo : lo + size] = sums[2 * ROWS :]
    for n, (lo, size) in enumerate(CUTS):
        a, b = came(0, 2, n, 0)
        onward(part[:ROWS, lo : lo + size] + a + b, 5, n, 2, 2)
        (a,) = came(2, 1, n, 1)
        onward(part[ROWS : 2 * ROWS, lo : lo + size] + a, 6, n, -2, 2)
    whole = []
    for n, (lo, size) in enumerate(CUTS):
        a, b, c, d = came(3, 4, n, 2)
        whole.append(part[2 * ROWS :, lo : lo + size] + (a + b) + (c + d))
    whole = jnp.concatenate(whole, axis=1)
    inverse = lax.rsqrt(whole[:, 2 * UNITS : 2 * UNITS + 1] * (1.0 / D) + 1e-06)
    gate = whole[:, :UNITS] * inverse
    up = whole[:, UNITS : 2 * UNITS] * inverse
    hid[z] = (gate / (1.0 + jnp.exp(-gate)) * up).astype(BF16)

    load_w[3].wait()
    swaps[3].wait_recv()
    gather(hid, hid_sem, project(hid, dw_v, d_out, d_in, d_sem, 1 - core), *HID_PLAN)
    lowered = collect(d_in, d_sem, owns_later)
    out[...] = (stream + lowered[:, :FEAT]).astype(BF16)

    for copy in swaps:
        copy.wait_send()
    left(head_out.at[pl.ds(0, PLANE - 1)], head_sem.at[0])
    gather_end(val, val_sem)
    others(o_out, o_sem.at[0], left, owns)
    others(x_in, x_sem.at[0], left, owns_later)
    for n, (lo, size) in enumerate(CUTS):
        left(sum_out.at[:, :, pl.ds(lo, size)], sum_send.at[n])
    gather_end(hid, hid_sem)
    others(d_out, d_sem.at[0], left, owns_later)


def layer(
    queries,
    new_latent,
    latent_cache,
    cached_lengths,
    value_up,
    out_weight,
    residual_in,
    norm_gain,
    gate_weight,
    up_weight,
    down_weight,
):
    anywhere = pl.BlockSpec(memory_space=pl.ANY)
    dma = pltpu.SemaphoreType.DMA
    return pl.pallas_call(
        kernel,
        out_shape=jax.ShapeDtypeStruct((ROWS, FEAT), BF16),
        in_specs=[anywhere] * 11,
        out_specs=pl.BlockSpec(memory_space=pltpu.VMEM),
        scratch_shapes=[
            pltpu.VMEM((KEY, HEADS), BF16),
            pltpu.VMEM((KEY, CACHE), BF16),
            pltpu.SMEM((1,), jnp.int32),
            pltpu.VMEM((1, KEY), BF16),
            pltpu.VMEM((ROWS, FEAT), BF16),
            pltpu.VMEM((1, FEAT), F32),
            pltpu.VMEM((LATENT, VALUES), BF16),
            pltpu.VMEM((2, FEAT, VALUES), BF16),
            pltpu.VMEM((2 * PAD, WIDE), BF16),
            pltpu.VMEM((2, FEAT, UNITS), BF16),
            pltpu.VMEM((PLANE, ROWS, LATENT // 2), BF16),
            pltpu.VMEM((PLANE, ROWS, LATENT // 2), BF16),
            pltpu.VMEM((CHIPS, ROWS, VALUES), BF16),
            pltpu.VMEM((PLANE, ROWS, PAD), BF16),
            pltpu.VMEM((PLANE, ROWS, PAD), BF16),
            pltpu.VMEM((ROWS, PAD), BF16),
            pltpu.VMEM((PLANE, ROWS, PAD), BF16),
            pltpu.VMEM((3 * ROWS, WIDE), F32),
            pltpu.VMEM((7, ROWS, WIDE), BF16),
            pltpu.VMEM((7, ROWS, WIDE), BF16),
            pltpu.VMEM((CHIPS, ROWS, UNITS), BF16),
            pltpu.VMEM((PLANE, ROWS, PAD), BF16),
            pltpu.VMEM((PLANE, ROWS, PAD), BF16),
            dma((11,)),
            dma((4,)),
            dma((4,)),
            dma((2,)),
            dma((4,)),
            dma((2,)),
            dma((2,)),
            dma((len(CUTS),)),
            dma((len(CUTS), 3)),
            dma((4,)),
            dma((2,)),
        ],
        compiler_params=pltpu.CompilerParams(
            collective_id=0, has_side_effects=True, vmem_limit_bytes=60 * 1024 * 1024
        ),
    )(
        queries.transpose(0, 2, 1),
        new_latent,
        latent_cache.transpose(0, 2, 1),
        cached_lengths,
        value_up,
        out_weight.T,
        residual_in,
        norm_gain.reshape(1, FEAT),
        gate_weight,
        up_weight,
        down_weight.T,
    )


def solution(mesh):
    in_specs = (
        P(("dp", "tp"), None, None),
        P(("dp", "tp"), None),
        P(("dp", "tp"), None, None),
        P(("dp", "tp")),
        P("tp", None, None),
        P("tp", "dp"),
        P("tp", "dp"),
        P("dp"),
        P("dp", "tp"),
        P("dp", "tp"),
        P("tp", "dp"),
    )
    return jax.shard_map(
        layer, mesh=mesh, in_specs=in_specs, out_specs=P("tp", "dp"), check_vma=False
    )
```

```python
import jax
import jax.numpy as jnp
from jax import lax
from jax.experimental import pallas as pl
from jax.experimental.pallas import tpu as pltpu
from jax.sharding import PartitionSpec as P

D = 7168
HEADS = 128
LATENT = 512
KEY = 576
CACHE = 1024
SCALE = (128 + 64) ** (-0.5)
PLANE = 16
CHIPS = 8
ROWS = 16
OWN_HEADS = 8
VALUES = 1024
FEAT = 448
PAD = 512
UNITS = 1152
WIDE = 2 * UNITS + 128
F32 = jnp.float32
BF16 = jnp.bfloat16
MESH = pl.DeviceIdType.MESH
FAR_FIRST = (10, 6, 9, 11, 14, 5, 7, 13, 15, 2, 8, 1, 3, 4, 12)
VAL_PLAN = ((1, 7, 2, 6, 3, 5, 4), {}, ((0,), (1, 7), (2, 6), (3, 5, 4)))
HID_PLAN = ((2, 6, 1, 7), {2: (2, 1), 6: (-1,)}, ((0,), (2, 6), (1, 7), (3, 5, 4)))
CUTS = ((0, 640), (640, 640), (1280, 640), (1920, WIDE - 1920))


def by_columns(a, b):
    return lax.dot_general(a, b, (((1,), (1,)), ((), ())), preferred_element_type=F32)


def kernel(
    queries,
    fresh,
    cache,
    length,
    value_up,
    out_weight,
    residual,
    gain,
    gate_weight,
    up_weight,
    down_weight,
    out,
    q_v,
    k_v,
    length_s,
    fresh_v,
    residual_v,
    gain_v,
    vu_v,
    ow_v,
    gu_v,
    dw_v,
    head_out,
    head_in,
    val,
    o_out,
    o_in,
    x_out,
    x_in,
    part,
    sum_out,
    sum_in,
    hid,
    d_out,
    d_in,
    load_sem,
    swap_send,
    swap_recv,
    head_sem,
    val_sem,
    o_sem,
    x_sem,
    sum_send,
    sum_recv,
    hid_sem,
    d_sem,
):
    dp, tp = lax.axis_index("dp"), lax.axis_index("tp")
    z, core = lax.div(dp, 2), lax.rem(dp, 2)
    way = 1 - 2 * core
    tp_chip, tp_core = lax.div(tp, 2), lax.rem(tp, 2)
    owns = core == tp_core
    owns_later = core != tp_core
    sibling = (dp + way, tp)

    def chip(steps):
        return lax.rem(z + way * steps + 2 * CHIPS, CHIPS)

    def along(steps):
        return (2 * chip(steps) + core, tp)

    def column(steps):
        return lax.rem(tp + steps, PLANE)


    def push(src, dst, send_sem, recv_sem, device):
        copy = pltpu.make_async_remote_copy(src, dst, send_sem, recv_sem, device, MESH)
        copy.start()
        return copy

    def landed(ref, sem):
        pltpu.make_async_remote_copy(ref, ref, sem, sem, sibling, MESH).wait_recv()

    def left(ref, sem):
        pltpu.make_async_remote_copy(ref, ref, sem, sem, sibling, MESH).wait_send()

    def others(ref, sem, wait, owned):
        @pl.when(owned)
        def _():
            wait(ref.at[pl.ds(0, PLANE - 1)], sem)

        @pl.when(jnp.logical_not(owned))
        def _():
            wait(ref, sem)

    def load(src, dst, i):
        copy = pltpu.make_async_copy(src, dst, load_sem.at[i])
        copy.start()
        return copy

    load_q = load(queries.at[0], q_v, 0)
    load_k = load(cache.at[0], k_v, 1)
    load_small = [
        load(fresh, fresh_v, 2),
        load(residual, residual_v, 3),
        load(gain, gain_v, 4),
        load(length, length_s, 10),
    ]

    barrier = pltpu.get_barrier_semaphore()
    for i in FAR_FIRST:
        pl.semaphore_signal(barrier, inc=1, device_id=(dp, column(i)), device_id_type=MESH)
    for i in range(PLANE):
        pl.semaphore_signal(
            barrier, inc=1, device_id=(dp + way, column(i)), device_id_type=MESH
        )
    for i in range(1, CHIPS):
        pl.semaphore_signal(barrier, inc=1, device_id=along(i), device_id_type=MESH)

    gu_v[FEAT:PAD, :] = jnp.zeros((PAD - FEAT, WIDE), BF16)
    gu_v[PAD + FEAT :, :] = jnp.zeros((PAD - FEAT, WIDE), BF16)
    gu_v[:, 2 * UNITS :] = jnp.zeros((2 * PAD, WIDE - 2 * UNITS), BF16)
    row = lax.broadcasted_iota(jnp.int32, (16, 128), 0)
    ones = jnp.where(row < 2, 1.0, 0.0).astype(BF16)
    gu_v[FEAT : FEAT + 16, 2 * UNITS :] = ones
    gu_v[PAD + FEAT : PAD + FEAT + 16, 2 * UNITS :] = ones

    load_q.wait()
    load_k.wait()
    for h in range(OWN_HEADS):
        load(value_up.at[h], vu_v.at[:, pl.ds(128 * h, 128)], 5)
    mine = pl.ds(pl.multiple_of(core * PAD, PAD), FEAT)
    weights = [
        (out_weight, ow_v.at[core]),
        (gate_weight, gu_v.at[mine, pl.ds(0, UNITS)]),
        (up_weight, gu_v.at[mine, pl.ds(UNITS, UNITS)]),
        (down_weight, dw_v.at[core]),
    ]
    load_w = [load(src, dst, 6 + i) for i, (src, dst) in enumerate(weights)]
    q = q_v[...].T
    scores = jnp.dot(q, k_v[...], preferred_element_type=F32)
    for copy in load_small:
        copy.wait()
    position = lax.broadcasted_iota(jnp.int32, (HEADS, CACHE), 1)
    scores = jnp.where(position < length_s[0], scores * SCALE, -1e30)
    new = fresh_v[...].astype(F32)
    own = jnp.sum(q.astype(F32) * new, axis=1, keepdims=True) * SCALE
    top = jnp.maximum(own, jnp.max(scores, axis=1, keepdims=True))
    weight = jnp.exp(scores - top)
    own_weight = jnp.exp(own - top)
    total = jnp.sum(weight, axis=1, keepdims=True) + own_weight
    summed = by_columns(weight.astype(BF16), k_v[:LATENT, :])
    latent = ((summed + own_weight * new[:, :LATENT]) / total).reshape(PLANE, OWN_HEADS, LATENT)
    half = LATENT // 2
    head_out[...] = jnp.concatenate([latent[:, :, :half], latent[:, :, half:]], axis=1).astype(BF16)

    pl.semaphore_wait(barrier, 2 * PLANE - 1 + CHIPS - 1)
    for i in FAR_FIRST:
        to = column(i)
        push(head_out.at[to], head_in.at[tp], head_sem.at[0], head_sem.at[1], (dp, to))
    swaps = [
        push(src, dst, swap_send.at[i], swap_recv.at[i], sibling)
        for i, (src, dst) in enumerate(weights)
    ]
    head_in[tp] = head_out[tp]
    pltpu.make_async_copy(vu_v, vu_v, load_sem.at[5]).wait()
    landed(head_in.at[pl.ds(0, PLANE - 1)], head_sem.at[1])

    wide = head_in[...].astype(F32)
    latents = jnp.concatenate([wide[:, :OWN_HEADS], wide[:, OWN_HEADS:]], axis=2)
    latents = latents.reshape(PLANE * OWN_HEADS, LATENT).astype(BF16)
    products = jnp.dot(latents, vu_v[...], preferred_element_type=F32)
    row_head = lax.broadcasted_iota(jnp.int32, products.shape, 0) & (OWN_HEADS - 1)
    column_head = lax.broadcasted_iota(jnp.int32, products.shape, 1) >> 7
    products = jnp.where(row_head == column_head, products, 0.0).astype(BF16)
    to_row = lax.broadcasted_iota(jnp.int32, (ROWS, PLANE * OWN_HEADS), 0)
    from_row = lax.broadcasted_iota(jnp.int32, (ROWS, PLANE * OWN_HEADS), 1) >> 3
    pick = jnp.where(to_row == from_row, 1.0, 0.0).astype(BF16)
    val[z] = jnp.dot(pick, products, preferred_element_type=F32).astype(BF16)

    def gather(buf, sem, use, order, relays, groups):
        def group_of(d):
            return [d % CHIPS in g for g in groups].index(True)

        for d in order:
            push(buf.at[z], buf.at[z], sem.at[0], sem.at[group_of(d)], along(d))
        for n, group in enumerate(groups):
            if n:
                landed(buf.at[pl.ds(0, len(group))], sem.at[n])
            for d in group:
                for step in relays.get(d, ()):
                    block = buf.at[chip(-d)]
                    push(block, block, sem.at[0], sem.at[group_of(d + step)], along(step))
            use([chip(-d) for d in group])

    def gather_end(buf, sem):
        left(buf.at[pl.ds(0, CHIPS - 1)], sem.at[0])

    def project(buf, w, dst_out, dst_in, sem, parity):
        def use(chips):
            rows = jnp.concatenate([buf[c] for c in chips], axis=0) if len(chips) > 1 else buf[chips[0]]
            for to in range(2):
                sums = by_columns(rows, w[to]).astype(BF16)
                for n, c in enumerate(chips):
                    dst_out[2 * c + to, :, :FEAT] = sums[n * ROWS : (n + 1) * ROWS]
                for c in chips:
                    block = dst_out.at[2 * c + to]
                    owner = 2 * c + parity
                    mine = jnp.logical_and(core == to, owner == tp)

                    @pl.when(jnp.logical_not(mine))
                    def _():
                        push(block, dst_in.at[tp], sem.at[0], sem.at[1], (2 * z + to, owner))

                    @pl.when(mine)
                    def _():
                        dst_in[tp] = block[...]

        return use

    def collect(dst_in, sem, owned):
        others(dst_in, sem.at[1], landed, owned)
        return jnp.sum(dst_in[...].astype(F32), axis=0)

    load_w[0].wait()
    swaps[0].wait_recv()
    gather(val, val_sem, project(val, ow_v, o_out, o_in, o_sem, core), *VAL_PLAN)
    attention = collect(o_in, o_sem, owns)
    stream = residual_v[...].astype(F32) + attention[:, :FEAT]

    squares = jnp.sum(stream * stream, axis=1, keepdims=True)
    high = squares.astype(BF16).astype(F32)
    lane = lax.broadcasted_iota(jnp.int32, (ROWS, PAD - FEAT), 1)
    extra = jnp.where(lane == 0, high, jnp.where(lane == 1, squares - high, 0.0))
    x_out[:, :FEAT] = (stream * gain_v[...]).astype(BF16)
    x_out[:, FEAT:] = extra.astype(BF16)
    slot = 2 * tp_chip + core
    for i in FAR_FIRST:
        push(x_out, x_in.at[slot], x_sem.at[0], x_sem.at[1], (2 * z + 1 - tp_core, column(i)))

    @pl.when(owns)
    def _():
        push(x_out, x_in.at[slot], x_sem.at[0], x_sem.at[1], sibling)

    @pl.when(owns_later)
    def _():
        x_in[slot] = x_out[...]

    for copy in load_w[1:3]:
        copy.wait()
    for copy in swaps[1:3]:
        copy.wait_recv()
    others(x_in, x_sem.at[1], landed, owns_later)

    def rows_for(steps):
        blocks = [
            jnp.concatenate([x_in[2 * chip(d)], x_in[2 * chip(d) + 1]], axis=1) for d in steps
        ]
        return jnp.concatenate(blocks, axis=0)

    def onward(value, i, n, device, group):
        lo, size = CUTS[n]
        cut = pl.ds(lo, size)
        sum_out[i, :, lo : lo + size] = value.astype(BF16)
        push(
            sum_out.at[i, :, cut],
            sum_in.at[i, :, cut],
            sum_send.at[n],
            sum_recv.at[n, group],
            along(device),
        )

    def came(first, count, n, group):
        lo, size = CUTS[n]
        landed(sum_in.at[pl.ds(first, count), :, pl.ds(lo, size)], sum_recv.at[n, group])
        return [sum_in[first + k, :, lo : lo + size].astype(F32) for k in range(count)]

    far, near = rows_for((4, 3, -3)), rows_for((1, -1, 2, -2, 0))
    for n, (lo, size) in enumerate(CUTS):
        sums = jnp.dot(far, gu_v[:, lo : lo + size], preferred_element_type=F32)
        onward(sums[:ROWS], 0, n, 2, 0)
        onward(sums[ROWS : 2 * ROWS], 1, n, 1, 0)
        onward(sums[2 * ROWS :], 2, n, -1, 1)
    for n, (lo, size) in enumerate(CUTS):
        sums = jnp.dot(near, gu_v[:, lo : lo + size], preferred_element_type=F32)
        onward(sums[:ROWS], 3, n, 1, 2)
        onward(sums[ROWS : 2 * ROWS], 4, n, -1, 2)
        part[:, lo : lo + size] = sums[2 * ROWS :]
    for n, (lo, size) in enumerate(CUTS):
        a, b = came(0, 2, n, 0)
        onward(part[:ROWS, lo : lo + size] + a + b, 5, n, 2, 2)
        (a,) = came(2, 1, n, 1)
        onward(part[ROWS : 2 * ROWS, lo : lo + size] + a, 6, n, -2, 2)
    whole = []
    for n, (lo, size) in enumerate(CUTS):
        a, b, c, d = came(3, 4, n, 2)
        whole.append(part[2 * ROWS :, lo : lo + size] + (a + b) + (c + d))
    whole = jnp.concatenate(whole, axis=1)
    inverse = lax.rsqrt(whole[:, 2 * UNITS : 2 * UNITS + 1] * (1.0 / D) + 1e-06)
    gate = whole[:, :UNITS] * inverse
    up = whole[:, UNITS : 2 * UNITS] * inverse
    hid[z] = (gate / (1.0 + jnp.exp(-gate)) * up).astype(BF16)

    load_w[3].wait()
    swaps[3].wait_recv()
    gather(hid, hid_sem, project(hid, dw_v, d_out, d_in, d_sem, 1 - core), *HID_PLAN)
    lowered = collect(d_in, d_sem, owns_later)
    out[...] = (stream + lowered[:, :FEAT]).astype(BF16)

    for copy in swaps:
        copy.wait_send()
    left(head_out.at[pl.ds(0, PLANE - 1)], head_sem.at[0])
    gather_end(val, val_sem)
    others(o_out, o_sem.at[0], left, owns)
    others(x_in, x_sem.at[0], left, owns_later)
    for n, (lo, size) in enumerate(CUTS):
        left(sum_out.at[:, :, pl.ds(lo, size)], sum_send.at[n])
    gather_end(hid, hid_sem)
    others(d_out, d_sem.at[0], left, owns_later)


def layer(
    queries,
    new_latent,
    latent_cache,
    cached_lengths,
    value_up,
    out_weight,
    residual_in,
    norm_gain,
    gate_weight,
    up_weight,
    down_weight,
):
    anywhere = pl.BlockSpec(memory_space=pl.ANY)
    dma = pltpu.SemaphoreType.DMA
    return pl.pallas_call(
        kernel,
        out_shape=jax.ShapeDtypeStruct((ROWS, FEAT), BF16),
        in_specs=[anywhere] * 11,
        out_specs=pl.BlockSpec(memory_space=pltpu.VMEM),
        scratch_shapes=[
            pltpu.VMEM((KEY, HEADS), BF16),
            pltpu.VMEM((KEY, CACHE), BF16),
            pltpu.SMEM((1,), jnp.int32),
            pltpu.VMEM((1, KEY), BF16),
            pltpu.VMEM((ROWS, FEAT), BF16),
            pltpu.VMEM((1, FEAT), F32),
            pltpu.VMEM((LATENT, VALUES), BF16),
            pltpu.VMEM((2, FEAT, VALUES), BF16),
            pltpu.VMEM((2 * PAD, WIDE), BF16),
            pltpu.VMEM((2, FEAT, UNITS), BF16),
            pltpu.VMEM((PLANE, ROWS, LATENT // 2), BF16),
            pltpu.VMEM((PLANE, ROWS, LATENT // 2), BF16),
            pltpu.VMEM((CHIPS, ROWS, VALUES), BF16),
            pltpu.VMEM((PLANE, ROWS, PAD), BF16),
            pltpu.VMEM((PLANE, ROWS, PAD), BF16),
            pltpu.VMEM((ROWS, PAD), BF16),
            pltpu.VMEM((PLANE, ROWS, PAD), BF16),
            pltpu.VMEM((3 * ROWS, WIDE), F32),
            pltpu.VMEM((7, ROWS, WIDE), BF16),
            pltpu.VMEM((7, ROWS, WIDE), BF16),
            pltpu.VMEM((CHIPS, ROWS, UNITS), BF16),
            pltpu.VMEM((PLANE, ROWS, PAD), BF16),
            pltpu.VMEM((PLANE, ROWS, PAD), BF16),
            dma((11,)),
            dma((4,)),
            dma((4,)),
            dma((2,)),
            dma((4,)),
            dma((2,)),
            dma((2,)),
            dma((len(CUTS),)),
            dma((len(CUTS), 3)),
            dma((4,)),
            dma((2,)),
        ],
        compiler_params=pltpu.CompilerParams(
            collective_id=0, has_side_effects=True, vmem_limit_bytes=60 * 1024 * 1024
        ),
    )(
        queries.transpose(0, 2, 1),
        new_latent,
        latent_cache.transpose(0, 2, 1),
        cached_lengths,
        value_up,
        out_weight.T,
        residual_in,
        norm_gain.reshape(1, FEAT),
        gate_weight,
        up_weight,
        down_weight.T,
    )


def solution(mesh):
    in_specs = (
        P(("dp", "tp"), None, None),
        P(("dp", "tp"), None),
        P(("dp", "tp"), None, None),
        P(("dp", "tp")),
        P("tp", None, None),
        P("tp", "dp"),
        P("tp", "dp"),
        P("dp"),
        P("dp", "tp"),
        P("dp", "tp"),
        P("tp", "dp"),
    )
    return jax.shard_map(
        layer, mesh=mesh, in_specs=in_specs, out_specs=P("tp", "dp"), check_vma=False
    )
```
